32 devices in a mesh: dp: 8 (over y, x, core), tensor: 4 (over z).
Axes of the slice: x: 2, y: 2, z: 4, core: 2. Of those that a mesh axis runs over, the one named last changes fastest.
Arguments:
- hidden_in: bfloat16 [16, 1024, 1024], P('dp', 'tensor'), may hold values from -6 to 6
- segments: int32 [16, 1024], P('dp'), may hold values from 0 to 2, as said below
- ln1_gain: bfloat16 [1024], replicated, may hold values from 0.5 to 1.5
- ln1_bias: bfloat16 [1024], replicated, may hold values from -3 to 3
- ln2_gain: bfloat16 [1024], replicated, may hold values from 0.5 to 1.5
- ln2_bias: bfloat16 [1024], replicated, may hold values from -3 to 3
- w_qkv: bfloat16 [3, 1024, 1024], P(None, 'dp', 'tensor'), may hold values from -0.1875 to 0.1875
- b_qkv: bfloat16 [3, 1024], replicated, may hold values from -6 to 6
- w_out: bfloat16 [1024, 1024], P('dp', 'tensor'), may hold values from -0.75 to 0.75
- b_out: bfloat16 [1024], replicated, may hold values from -4 to 4
- w_up: bfloat16 [1024, 4096], P('dp', 'tensor'), may hold values from -0.1875 to 0.1875
- b_up: bfloat16 [4096], replicated, may hold values from -6 to 6
- w_down: bfloat16 [1024, 4096], P('dp', 'tensor'), may hold values from -0.09375 to 0.09375
- b_down: bfloat16 [1024], replicated, may hold values from -4 to 4
- cotangent: bfloat16 [16, 1024, 1024], P('dp', 'tensor'), may hold values from -6 to 6
Outputs:
- block_out: bfloat16 [16, 1024, 1024], P('dp', 'tensor')
- grad_in: bfloat16 [16, 1024, 1024], P('dp', 'tensor')
- grad_ln1_gain: float32 [1024], replicated
- grad_ln1_bias: float32 [1024], replicated
- grad_ln2_gain: float32 [1024], replicated
- grad_ln2_bias: float32 [1024], replicated
- grad_w_qkv: float32 [3, 1024, 1024], P(None, 'dp', 'tensor')
- grad_b_qkv: float32 [3, 1024], replicated
- grad_w_out: float32 [1024, 1024], P('dp', 'tensor')
- grad_b_out: float32 [1024], replicated
- grad_w_up: float32 [1024, 4096], P('dp', 'tensor')
- grad_b_up: float32 [4096], replicated
- grad_w_down: float32 [1024, 4096], P('dp', 'tensor')
- grad_b_down: float32 [1024], replicated
The draws below stay inside these ranges and needn't reach their ends.
Inputs may be any that keep to these rules, and one draw needn't show every extreme that they name: `segments`: segment numbers start at 0 in every sequence and never fall along it; of the 2 sequences of each index of dp, one holds a single document.
All inputs are finite; a program needn't handle non-finite values.
Results may differ from the reference program's by a relative error of at most 0.0097.
Values may be sent and summed in bfloat16 or wider, within the bound.
A program may use at most 128 MiB of HBM per device.

```python
import math
import jax
import jax.numpy as jnp
from jax import lax

D = 1024
HEADS = 16
HEAD_DIM = 64
ROT = 16
FF = 4096
LEN = 1024
SEQ_DEV = 2
SEQS = 16


def draw_segments(key, part):
    key = jax.random.fold_in(key, 7)
    first_key, second_key, whole_key = jax.random.split(key, 3)
    groups = SEQS // SEQ_DEV
    first_cut = jax.random.randint(first_key, (SEQS, 1), LEN // 8, 3 * LEN // 8)
    second_cut = first_cut + jax.random.randint(second_key, (SEQS, 1), LEN // 5, 2 * LEN // 5)
    places = jnp.arange(LEN, dtype=jnp.int32)[None, :]
    numbers = (places >= first_cut).astype(jnp.int32) + (places >= second_cut).astype(jnp.int32)
    chosen = jax.random.randint(whole_key, (groups, 1), 0, SEQ_DEV)
    single = (jnp.arange(SEQ_DEV, dtype=jnp.int32)[None, :] == chosen).reshape(SEQS)
    return jnp.where(single[:, None], 0, numbers).astype(jnp.int32)


def raised(array, stream_key, source, target, shards_of, factor):
    def block_of(axis_at):
        return (jnp.arange(array.shape[axis_at]) // (array.shape[axis_at] // shards_of)).reshape((-1,) + (1,) * (array.ndim - 1 - axis_at))

    near = jax.random.permutation(stream_key, shards_of)[block_of(target)]
    other_side = (block_of(target) + shards_of // 2) % shards_of
    return jnp.where((block_of(source) == near) | (block_of(source) == other_side), factor * array, array)


def level_of(rng, shape, cuts, smallest, largest):
    loudness = 1.0
    for axis_at, blocks in cuts:
        heights = jax.random.uniform(jax.random.fold_in(jax.random.fold_in(rng, 6), axis_at), (blocks,), jnp.float32, smallest / len(cuts), largest / len(cuts))
        loudness = loudness * jnp.repeat(jnp.exp(heights), shape[axis_at] // blocks).reshape((-1,) + (1,) * (len(shape) - 1 - axis_at))
    return loudness


def scatter_about(stream_key, dims, deviation, reach, pieces=(), kind=jnp.bfloat16):
    gain = level_of(stream_key, dims, pieces, -0.22, 0.18) if pieces else 1.0
    array = jax.random.normal(stream_key, dims, jnp.float32) * deviation * gain
    return jnp.minimum(jnp.maximum(array, -reach), reach).astype(kind)


def heavy_noise(rng, dims, scale, reach, pieces, heavy, kind=jnp.bfloat16):
    drawn = scale * jax.random.normal(rng, dims, jnp.float32)
    if pieces:
        drawn = drawn * level_of(rng, dims, pieces, -0.22, 0.18)
    return jnp.clip(raised(drawn, jax.random.fold_in(rng, 3), *heavy), -reach, reach).astype(kind)


def setup_inputs(seed: int = 0) -> dict:
    splits = jax.random.split(jax.random.key(seed), 16)
    return {
        "hidden_in": scatter_about(splits[0], (SEQS, LEN, D), 1.0, 6.0, ((0, 8), (1, 4))),
        "segments": draw_segments(jax.random.fold_in(splits[15], 71), 0),
        "ln1_gain": jnp.clip(1.0 + 0.1 * jax.random.normal(splits[2], (D,), jnp.float32), 0.5, 1.5).astype(jnp.bfloat16),
        "ln1_bias": scatter_about(splits[3], (D,), 0.2, 3.0),
        "ln2_gain": jnp.clip(1.0 + 0.1 * jax.random.normal(splits[4], (D,), jnp.float32), 0.5, 1.5).astype(jnp.bfloat16),
        "ln2_bias": scatter_about(splits[5], (D,), 0.2, 3.0),
        "w_qkv": scatter_about(splits[6], (3, D, D), D ** -0.5, 0.1875, ((1, 8), (2, 4))),
        "b_qkv": scatter_about(splits[7], (3, D), 0.5, 6.0),
        "w_out": scatter_about(splits[8], (D, D), (D // 16) ** -0.5, 0.75, ((0, 8), (1, 4))),
        "b_out": scatter_about(splits[9], (D,), 0.3, 4.0),
        "w_up": scatter_about(splits[10], (D, FF), D ** -0.5, 0.1875, ((0, 8), (1, 4))),
        "b_up": scatter_about(splits[11], (FF,), 0.5, 6.0),
        "w_down": scatter_about(splits[12], (D, FF), FF ** -0.5, 0.09375, ((0, 8), (1, 4))),
        "b_down": scatter_about(splits[13], (D,), 0.3, 4.0),
        "cotangent": heavy_noise(splits[14], (SEQS, LEN, D), 1.0, 6.0, ((0, 8), (1, 4)), (0, 2, 8, 2.0)),
    }


@jax.custom_vjp
def low(v):
    return lax.optimization_barrier(v.astype(jnp.bfloat16)).astype(jnp.float32)

@jax.custom_vjp
def low_back(v):
    return v

def low_keep(v):
    return (low(v), None)

def low_pass(kept, grad):
    return (grad,)

def back_keep(v):
    return (v, None)

def back_low(kept, grad):
    return (low(grad),)
low.defvjp(low_keep, low_pass)
low_back.defvjp(back_keep, back_low)
EPSILON = 1e-05
HIGHEST_PRECISION = lax.Precision.HIGHEST

def doc_positions(segment_ids):
    length_all = segment_ids.shape[-1]
    places = jnp.broadcast_to(jnp.arange(length_all, dtype=jnp.int32), segment_ids.shape)
    first_flag = jnp.ones(segment_ids.shape[:-1] + (1,), jnp.bool_)
    starts = jnp.concatenate([first_flag, segment_ids[..., 1:] != segment_ids[..., :-1]], -1)
    begins = lax.cummax(jnp.where(starts, places, 0).astype(jnp.int32), axis=segment_ids.ndim - 1)
    return (places - begins).astype(jnp.int32)

def rotary_tables(positions):
    frequency = 10000.0 ** (-jnp.arange(ROT // 2, dtype=jnp.float32) * (2.0 / ROT))
    angles = positions.astype(jnp.float32)[..., None] * frequency
    return (jnp.cos(angles)[..., None, :], jnp.sin(angles)[..., None, :])

def rotate(vectors, cosine_table, sine_table, direction):
    first_half = vectors[..., :ROT // 2]
    second_half = vectors[..., ROT // 2:ROT]
    untouched = vectors[..., ROT:]
    return jnp.concatenate([first_half * cosine_table - direction * second_half * sine_table, second_half * cosine_table + direction * first_half * sine_table, untouched], -1)

def one_sequence(params, hidden, segment_ids):
    ln1_gain, ln1_bias, ln2_gain, ln2_bias, w_qkv, b_qkv, w_out, b_out, w_up, b_up, w_down, b_down = params
    centred = hidden - lax.optimization_barrier(jnp.mean(hidden, -1, keepdims=True))
    normed = centred * lax.rsqrt(lax.optimization_barrier(jnp.mean(centred * centred, -1, keepdims=True)) + EPSILON)
    first_in = low(normed * ln1_gain + ln1_bias)
    second_in = low(normed * ln2_gain + ln2_bias)
    projected = low_back(jnp.einsum('ld,cde->cle', first_in, w_qkv, precision=HIGHEST_PRECISION) + b_qkv[:, None, :])
    cosine_table, sine_table = rotary_tables(doc_positions(segment_ids))
    head_shape = (LEN, HEADS, HEAD_DIM)
    queries = low(rotate(projected[0].reshape(head_shape), cosine_table, sine_table, 1.0) * (1.0 / math.sqrt(HEAD_DIM)))
    keys_all = low(rotate(projected[1].reshape(head_shape), cosine_table, sine_table, 1.0))
    values = low(projected[2].reshape(head_shape))
    scores = low_back(jnp.einsum('ihd,jhd->hij', queries, keys_all, precision=HIGHEST_PRECISION))
    places = jnp.arange(LEN, dtype=jnp.int32)
    allowed = (places[None, :] <= places[:, None]) & (segment_ids[None, :] == segment_ids[:, None])
    weights = low(jax.nn.softmax(jnp.where(allowed[None], scores, -1e+30), axis=-1))
    attended = jnp.einsum('hij,jhd->ihd', weights, values, precision=HIGHEST_PRECISION).reshape(LEN, D)
    attended = low(low_back(attended))
    units = low_back(jnp.dot(second_in, w_up, precision=HIGHEST_PRECISION) + b_up)
    activated = low(jax.nn.gelu(units, approximate=False))
    attention_part = jnp.dot(attended, w_out.T, precision=HIGHEST_PRECISION) + b_out
    forward_part = jnp.dot(activated, w_down.T, precision=HIGHEST_PRECISION) + b_down
    return hidden + attention_part + forward_part

def reference(hidden_in, segments, ln1_gain, ln1_bias, ln2_gain, ln2_bias, w_qkv, b_qkv, w_out, b_out, w_up, b_up, w_down, b_down, cotangent):
    params = tuple((member.astype(jnp.float32) for member in (ln1_gain, ln1_bias, ln2_gain, ln2_bias, w_qkv, b_qkv, w_out, b_out, w_up, b_up, w_down, b_down)))

    def forward(params_all, hidden_all):

        def advance(running, members):
            return (running, jax.checkpoint(one_sequence)(params_all, members[0], members[1]))
        _, outputs = lax.scan(advance, jnp.zeros((), jnp.float32), (hidden_all, segments))
        return outputs
    result, pullback = jax.vjp(forward, params, hidden_in.astype(jnp.float32))
    grad_params, grad_hidden = pullback(cotangent.astype(jnp.float32))
    return (result.astype(jnp.bfloat16), grad_hidden.astype(jnp.bfloat16), grad_params[0], grad_params[1], grad_params[2], grad_params[3], grad_params[4], grad_params[5], grad_params[6], grad_params[7], grad_params[8], grad_params[9], grad_params[10], grad_params[11])
```

```python
import math

import jax
import jax.numpy as jnp
from jax import lax
from jax.experimental import pallas as pl
from jax.experimental.pallas import tpu as pltpu
from jax.sharding import PartitionSpec as P

HEAD_DIM = 64
ROT = 16
PAIR = 2 * HEAD_DIM
ROWS = 256

EPSILON = 1e-05
BY_COLUMNS = (((1,), (1,)), ((), ()))
BY_ROWS = (((0,), (0,)), ((), ()))
F32 = jnp.float32
BF16 = jnp.bfloat16


def shifted(array, axis_name, size, shift):
    return lax.ppermute(array, axis_name, [(i, (i + shift) % size) for i in range(size)])


def swapped(array, axis_name, size, bit):
    return lax.ppermute(array, axis_name, [(i, i ^ bit) for i in range(size)])


def gather_tokens(block, axis_name, size, me):
    whole = jnp.zeros((block.shape[0], size) + block.shape[1:], block.dtype)
    pieces = [block] + [shifted(block, axis_name, size, k) for k in range(1, size)]
    for k, piece in enumerate(pieces):
        owner = lax.rem(me - k + size, size)
        whole = lax.dynamic_update_slice_in_dim(whole, piece[:, None], owner, 1)
    return whole


def scatter_tokens(parts, axis_name, size, me):
    def part_for(owner):
        return lax.dynamic_index_in_dim(parts, owner, 1, keepdims=False)

    total = part_for(me).astype(F32)
    for k in range(1, size):
        sent = part_for(lax.rem(me + k, size)).astype(BF16)
        total = total + shifted(sent, axis_name, size, k).astype(F32)
    return total


def bits_of(size):
    return [1 << i for i in range(size.bit_length() - 1)]


def gather_rows(block, axis_name, size, me, order):
    held = block
    for bit in order:
        other = swapped(held, axis_name, size, bit)
        upper = (me & bit) != 0
        held = jnp.stack([jnp.where(upper, other, held), jnp.where(upper, held, other)])
    axes = list(reversed(order))
    wanted = [axes.index(bit) for bit in reversed(bits_of(size))]
    count = len(order)
    held = held.transpose(wanted + list(range(count, held.ndim)))
    return held.reshape((size,) + block.shape)


def scatter_rows(parts, axis_name, size, me, order):
    bits = list(reversed(bits_of(size)))
    held = parts.reshape((2,) * len(bits) + parts.shape[1:])
    for bit in order:
        at = bits.index(bit)
        mine = (me // bit) % 2
        keep = lax.dynamic_index_in_dim(held, mine, at, keepdims=False)
        give = lax.dynamic_index_in_dim(held, 1 - mine, at, keepdims=False)
        held = keep + swapped(give.astype(BF16), axis_name, size, bit).astype(F32)
        bits.pop(at)
    return held


def sum_everywhere(vector, axes):
    for axis_name, size in axes:
        for bit in bits_of(size):
            vector = vector + swapped(vector, axis_name, size, bit)
    return vector


def attention_kernel(
    projected_ref, grad_ref, cos_ref, sin_ref, start_ref, out_ref, grads_ref,
    queries_t, outputs_t, keys_sum, values_sum,
):
    length = cos_ref.shape[1]
    block = min(ROWS, length)
    scale = 1.0 / math.sqrt(HEAD_DIM)
    cosine, sine = cos_ref[0], sin_ref[0]
    lanes = lax.broadcasted_iota(jnp.int32, (length, PAIR), 1)
    low = lax.rem(lanes, HEAD_DIM) < ROT // 2

    def partner(u):
        return jnp.where(low, pltpu.roll(u, PAIR - ROT // 2, 1), pltpu.roll(u, ROT // 2, 1))

    def rot(u):
        return u * cosine + partner(u) * sine

    def rot_back(u):
        return u * cosine - partner(u) * sine

    queries = (rot(projected_ref[0, 0]) * scale).astype(BF16)
    rotated = rot(projected_ref[1, 0])
    keys = rotated.astype(BF16)
    keys_t = rotated.T.astype(BF16)
    values = projected_ref[2, 0].astype(BF16)
    values_t = projected_ref[2, 0].T.astype(BF16)
    grads = grad_ref[0]

    keys_sum[...] = jnp.zeros_like(keys_sum)
    values_sum[...] = jnp.zeros_like(values_sum)
    for head in range(2):
        columns = slice(head * HEAD_DIM, (head + 1) * HEAD_DIM)
        for at in range(0, length, block):
            rows = slice(at, at + block)
            seen = at + block
            query, grad = queries[rows, columns], grads[rows, columns]
            scores = lax.dot_general(keys[:seen, columns], query, BY_COLUMNS, preferred_element_type=F32)
            key_at = lax.broadcasted_iota(jnp.int32, (seen, block), 0)
            query_at = at + lax.broadcasted_iota(jnp.int32, (seen, block), 1)
            allowed = (key_at >= start_ref[0, :, rows]) & (key_at <= query_at)
            scores = jnp.where(allowed, scores, -1e30)
            powered = jnp.exp(scores - jnp.max(scores, 0, keepdims=True))
            probabilities = powered * (1.0 / jnp.sum(powered, 0, keepdims=True))
            weights = probabilities.astype(BF16)
            outputs_t[columns, rows] = jnp.dot(
                values_t[columns, :seen], weights, preferred_element_type=F32
            )
            grad_probs = lax.dot_general(
                values[:seen, columns], grad, BY_COLUMNS, preferred_element_type=F32
            )
            inner = jnp.sum(probabilities * grad_probs, 0, keepdims=True)
            grad_scores = (probabilities * (grad_probs - inner)).astype(BF16)
            queries_t[columns, rows] = jnp.dot(
                keys_t[columns, :seen], grad_scores, preferred_element_type=F32
            )
            keys_sum[:seen, columns] += jnp.dot(grad_scores, query, preferred_element_type=F32)
            values_sum[:seen, columns] += jnp.dot(weights, grad, preferred_element_type=F32)
    out_ref[0] = outputs_t[...].T.astype(BF16)
    grads_ref[0, 0] = (rot_back(queries_t[...].T) * scale).astype(BF16)
    grads_ref[1, 0] = rot_back(keys_sum[...]).astype(BF16)
    grads_ref[2, 0] = values_sum[...].astype(BF16)


def attention(projected, grad_attended, cosine, sine, starts):
    _, count, length, width = projected.shape
    pairs = width // PAIR
    work = count * length * length * width
    return pl.pallas_call(
        attention_kernel,
        grid=(count, pairs),
        out_shape=(
            jax.ShapeDtypeStruct((count, length, width), BF16),
            jax.ShapeDtypeStruct((3, count, length, width), BF16),
        ),
        in_specs=[
            pl.BlockSpec((3, 1, length, PAIR), lambda s, h: (0, s, 0, h)),
            pl.BlockSpec((1, length, PAIR), lambda s, h: (s, 0, h)),
            pl.BlockSpec((1, length, PAIR), lambda s, h: (s, 0, 0)),
            pl.BlockSpec((1, length, PAIR), lambda s, h: (s, 0, 0)),
            pl.BlockSpec((1, 1, length), lambda s, h: (s, 0, 0)),
        ],
        out_specs=(
            pl.BlockSpec((1, length, PAIR), lambda s, h: (s, 0, h)),
            pl.BlockSpec((3, 1, length, PAIR), lambda s, h: (0, s, 0, h)),
        ),
        scratch_shapes=[
            pltpu.VMEM((PAIR, length), F32),
            pltpu.VMEM((PAIR, length), F32),
            pltpu.VMEM((length, PAIR), F32),
            pltpu.VMEM((length, PAIR), F32),
        ],
        compiler_params=pltpu.CompilerParams(vmem_limit_bytes=48 * 1024 * 1024),
        cost_estimate=pl.CostEstimate(
            flops=30 * work, bytes_accessed=24 * count * length * width,
            transcendentals=work // (2 * HEAD_DIM),
        ),
        name="attention",
    )(projected, grad_attended, cosine, sine, starts)


def make_shards(dp_size, tensor_size):
    def shards(
        hidden_in, segments, ln1_gain, ln1_bias, ln2_gain, ln2_bias, w_qkv, b_qkv,
        w_out, b_out, w_up, b_up, w_down, b_down, cotangent,
    ):
        count, own_length, width = hidden_in.shape
        length = segments.shape[1]
        rows = count * length
        dp_index, tensor_index = lax.axis_index("dp"), lax.axis_index("tensor")
        local = w_qkv.shape[2]
        local_units = w_up.shape[1]
        bits = bits_of(dp_size)
        order_a = bits[1:] + bits[:1]
        order_b = bits[:0:-1] + bits[:1]

        def gather(block):
            return gather_tokens(block, "tensor", tensor_size, tensor_index).reshape(rows, width)

        def scatter(parts):
            parts = parts.reshape(count, tensor_size, own_length, width)
            return scatter_tokens(parts, "tensor", tensor_size, tensor_index)

        hidden_rows = gather(hidden_in)
        attn_w = jnp.concatenate([w_qkv, w_out[None]], 0)
        attn_full = gather_rows(attn_w, "dp", dp_size, dp_index, order_a)
        full_qkv = attn_full[:, :3].transpose(1, 0, 2, 3).reshape(3, width, local)
        full_out = attn_full[:, 3].reshape(width, local)
        full_up = gather_rows(w_up, "dp", dp_size, dp_index, order_b).reshape(width, local_units)
        cot_rows = gather(cotangent)
        full_down = gather_rows(w_down, "dp", dp_size, dp_index, order_a).reshape(width, local_units)

        zeros = jnp.sum((segments == 0).astype(jnp.int32), -1, keepdims=True)
        ones = jnp.sum((segments == 1).astype(jnp.int32), -1, keepdims=True)
        starts = jnp.where(segments >= 1, zeros, 0) + jnp.where(segments >= 2, ones, 0)
        positions = jnp.arange(length, dtype=jnp.int32)[None] - starts
        place = jnp.arange(PAIR, dtype=jnp.int32) % HEAD_DIM
        frequency = 10000.0 ** (-(place % (ROT // 2)).astype(F32) * (2.0 / ROT))
        angles = positions.astype(F32)[..., None] * frequency
        cosine = jnp.where(place < ROT, jnp.cos(angles), 1.0)
        sines = jnp.sin(angles)
        sine = jnp.where(place < ROT // 2, -sines, jnp.where(place < ROT, sines, 0.0))

        def layer_normed(hidden):
            centred = hidden - jnp.mean(hidden, -1, keepdims=True)
            scaling = lax.rsqrt(jnp.mean(centred * centred, -1, keepdims=True) + EPSILON)
            return centred * scaling, scaling

        normed, _ = layer_normed(hidden_rows.astype(F32))
        first = (normed * ln1_gain + ln1_bias).astype(BF16)
        second = (normed * ln2_gain + ln2_bias).astype(BF16)
        bias_qkv = lax.dynamic_slice_in_dim(b_qkv, tensor_index * local, local, 1)
        bias_up = lax.dynamic_slice_in_dim(b_up, tensor_index * local_units, local_units, 0)

        projected = (
            jnp.einsum("rd,cde->cre", first, full_qkv, preferred_element_type=F32)
            + bias_qkv[:, None, :]
        )
        grad_attended = jnp.dot(cot_rows, full_out, preferred_element_type=F32).astype(BF16)
        attended, grad_projected = attention(
            projected.reshape(3, count, length, local),
            grad_attended.reshape(count, length, local),
            cosine, sine, starts[:, None, :],
        )
        attended = attended.reshape(rows, local)
        grad_projected = grad_projected.reshape(3, rows, local)

        units = jnp.dot(second, full_up, preferred_element_type=F32) + bias_up
        cumulative = 0.5 * (1.0 + lax.erf(units * (1.0 / math.sqrt(2.0))))
        density = jnp.exp(-0.5 * units * units) * (1.0 / math.sqrt(2.0 * math.pi))
        activated = (units * cumulative).astype(BF16)
        slope = cumulative + units * density
        grad_units = (jnp.dot(cot_rows, full_down, preferred_element_type=F32) * slope).astype(BF16)

        branch = lax.dot_general(attended, full_out, BY_COLUMNS, preferred_element_type=F32)
        branch = branch + lax.dot_general(activated, full_down, BY_COLUMNS, preferred_element_type=F32)
        hidden = hidden_in.astype(F32)
        block_out = (hidden + scatter(branch) + b_out + b_down).astype(BF16)

        grad_first = jnp.einsum("cre,cde->rd", grad_projected, full_qkv, preferred_element_type=F32)
        grad_second = lax.dot_general(grad_units, full_up, BY_COLUMNS, preferred_element_type=F32)
        norm_terms = [
            jnp.sum(grad_first * normed, 0), jnp.sum(grad_first, 0),
            jnp.sum(grad_second * normed, 0), jnp.sum(grad_second, 0),
        ]
        e = scatter(grad_first * ln1_gain + grad_second * ln2_gain)
        own_normed, own_scaling = layer_normed(hidden)
        grad_in = cotangent.astype(F32) + own_scaling * (
            e
            - jnp.mean(e, -1, keepdims=True)
            - own_normed * jnp.mean(e * own_normed, -1, keepdims=True)
        )

        def to_owners(part, order):
            split = part.reshape((dp_size, part.shape[0] // dp_size) + part.shape[1:])
            return scatter_rows(split, "dp", dp_size, dp_index, bits[:1] + order)

        xy, yx = bits[1:], bits[:0:-1]
        grad_w_down = to_owners(lax.dot_general(cot_rows, activated, BY_ROWS, preferred_element_type=F32), xy)
        grad_w_out = to_owners(lax.dot_general(cot_rows, attended, BY_ROWS, preferred_element_type=F32), xy)
        grad_w_up = to_owners(lax.dot_general(second, grad_units, BY_ROWS, preferred_element_type=F32), yx)
        grad_w_qkv = jnp.stack([
            to_owners(lax.dot_general(first, grad_projected[c], BY_ROWS, preferred_element_type=F32), yx if c else xy)
            for c in range(3)
        ])

        padded_qkv = lax.dynamic_update_slice_in_dim(
            jnp.zeros((3, width), F32), jnp.sum(grad_projected, 1, dtype=F32), tensor_index * local, 1
        )
        padded_up = lax.dynamic_update_slice_in_dim(
            jnp.zeros(b_up.shape, F32), jnp.sum(grad_units, 0, dtype=F32), tensor_index * local_units, 0
        )
        cot_sums = jnp.sum(cotangent, (0, 1), dtype=F32)
        vector = jnp.concatenate(norm_terms + [padded_qkv.reshape(-1), cot_sums, padded_up])
        vector = vector.reshape(-1, 128)
        vector = sum_everywhere(vector, (("tensor", tensor_size), ("dp", dp_size))).reshape(-1)
        g1, b1, g2, b2, qkv, cot_sum, up = jnp.split(
            vector, [width, 2 * width, 3 * width, 4 * width, 7 * width, 8 * width]
        )
        return (
            block_out, grad_in.astype(BF16), g1, b1, g2, b2, grad_w_qkv, qkv.reshape(3, width),
            grad_w_out, cot_sum, grad_w_up, up, grad_w_down, cot_sum,
        )

    return shards


def solution(mesh):
    tokens = P("dp", "tensor", None)
    weight = P("dp", "tensor")
    stacked = P(None, "dp", "tensor")
    in_specs = (
        tokens, P("dp", None), P(), P(), P(), P(), stacked, P(),
        weight, P(), weight, P(), weight, P(), tokens,
    )
    out_specs = (
        tokens, tokens, P(), P(), P(), P(), stacked, P(),
        weight, P(), weight, P(), weight, P(),
    )
    shards = make_shards(mesh.shape["dp"], mesh.shape["tensor"])
    return jax.shard_map(shards, mesh=mesh, in_specs=in_specs, out_specs=out_specs, check_vma=False)
```

```python
import math

import jax
import jax.numpy as jnp
from jax import lax
from jax.experimental import pallas as pl
from jax.experimental.pallas import tpu as pltpu
from jax.sharding import PartitionSpec as P

HEAD_DIM = 64
ROT = 16
PAIR = 2 * HEAD_DIM
ROWS = 256

EPSILON = 1e-05
BY_COLUMNS = (((1,), (1,)), ((), ()))
BY_ROWS = (((0,), (0,)), ((), ()))
F32 = jnp.float32
BF16 = jnp.bfloat16


def moved(array, axis_name, pairs):
    return lax.ppermute(array, axis_name, pairs)


def swapped(array, axis_name, size, bit):
    return lax.ppermute(array, axis_name, [(i, i ^ bit) for i in range(size)])


def gather_tokens(block, axis_name, size, me):
    from_left, from_right = [block], [block]
    for k in range(1, size):
        right = [(i, i + 1) for i in range(k - 1, size - 1)]
        left = [(i + 1, i) for i in range(size - k)]
        from_left.append(moved(from_left[-1], axis_name, right))
        from_right.append(moved(from_right[-1], axis_name, left))
    whole = jnp.zeros((block.shape[0], size) + block.shape[1:], block.dtype)
    for k in range(size):
        piece = block if k == 0 else jnp.where(me >= k, from_left[k], from_right[size - k])
        owner = lax.rem(me - k + size, size)
        whole = lax.dynamic_update_slice_in_dim(whole, piece[:, None], owner, 1)
    return whole


def scatter_tokens(parts, axis_name, size, me, between=None):
    def part_for(owner):
        return lax.dynamic_index_in_dim(parts, jnp.clip(owner, 0, size - 1), 1, keepdims=False).astype(F32)

    from_left = from_right = None
    for step in range(1, size):
        to_right, to_left = part_for(size - step + me), part_for(step - size + me)
        if step > 1:
            to_right, to_left = to_right + from_left.astype(F32), to_left + from_right.astype(F32)
        right = [(i, i + 1) for i in range(step)]
        left = [(size - 1 - i, size - 2 - i) for i in range(step)]
        from_left = moved(to_right.astype(BF16), axis_name, right)
        from_right = moved(to_left.astype(BF16), axis_name, left)
        if between is not None:
            from_left, from_right = between(step, from_left, from_right)
    return part_for(me) + from_left.astype(F32) + from_right.astype(F32)


def bits_of(size):
    return [1 << i for i in range(size.bit_length() - 1)]


def gather_rows(block, axis_name, size, me, order):
    held = block
    for bit in order:
        other = swapped(held, axis_name, size, bit)
        upper = (me & bit) != 0
        held = jnp.stack([jnp.where(upper, other, held), jnp.where(upper, held, other)])
    axes = list(reversed(order))
    wanted = [axes.index(bit) for bit in reversed(bits_of(size))]
    count = len(order)
    held = held.transpose(wanted + list(range(count, held.ndim)))
    return held.reshape((size,) + block.shape)


def scatter_rows(parts, axis_name, size, me, order):
    bits = list(reversed(bits_of(size)))
    held = parts.reshape((2,) * len(bits) + parts.shape[1:])
    for bit in order:
        at = bits.index(bit)
        mine = (me // bit) % 2
        keep = lax.dynamic_index_in_dim(held, mine, at, keepdims=False)
        give = lax.dynamic_index_in_dim(held, 1 - mine, at, keepdims=False)
        held = keep + swapped(give.astype(BF16), axis_name, size, bit).astype(F32)
        bits.pop(at)
    return held


def sum_stages(axes):
    return [(axis_name, size, bit) for axis_name, size in axes for bit in bits_of(size)]


def attention_kernel(
    query_ref, key_ref, value_ref, grad_ref, cos_ref, sin_ref, start_ref,
    out_ref, grad_query_ref, grad_key_ref, grad_value_ref,
    queries_t, outputs_t, keys_sum, values_sum,
):
    length = cos_ref.shape[1]
    block = min(ROWS, length)
    scale = 1.0 / math.sqrt(HEAD_DIM)
    cosine, sine = cos_ref[0], sin_ref[0]
    lanes = lax.broadcasted_iota(jnp.int32, (length, PAIR), 1)
    low = lax.rem(lanes, HEAD_DIM) < ROT // 2

    def partner(u):
        return jnp.where(low, pltpu.roll(u, PAIR - ROT // 2, 1), pltpu.roll(u, ROT // 2, 1))

    def rot(u):
        return u * cosine + partner(u) * sine

    def rot_back(u):
        return u * cosine - partner(u) * sine

    queries = (rot(query_ref[0]) * scale).astype(BF16)
    rotated = rot(key_ref[0])
    keys = rotated.astype(BF16)
    keys_t = rotated.T.astype(BF16)
    values = value_ref[0].astype(BF16)
    values_t = value_ref[0].T.astype(BF16)
    grads = grad_ref[0]

    keys_sum[...] = jnp.zeros_like(keys_sum)
    values_sum[...] = jnp.zeros_like(values_sum)
    for head in range(2):
        columns = slice(head * HEAD_DIM, (head + 1) * HEAD_DIM)
        for at in range(0, length, block):
            rows = slice(at, at + block)
            seen = at + block
            query, grad = queries[rows, columns], grads[rows, columns]
            scores = lax.dot_general(keys[:seen, columns], query, BY_COLUMNS, preferred_element_type=F32)
            key_at = lax.broadcasted_iota(jnp.int32, (seen, block), 0)
            query_at = at + lax.broadcasted_iota(jnp.int32, (seen, block), 1)
            allowed = (key_at >= start_ref[0, :, rows]) & (key_at <= query_at)
            scores = jnp.where(allowed, scores, -1e30)
            powered = jnp.exp(scores - jnp.max(scores, 0, keepdims=True))
            probabilities = powered * (1.0 / jnp.sum(powered, 0, keepdims=True))
            weights = probabilities.astype(BF16)
            outputs_t[columns, rows] = jnp.dot(
                values_t[columns, :seen], weights, preferred_element_type=F32
            )
            grad_probs = lax.dot_general(
                values[:seen, columns], grad, BY_COLUMNS, preferred_element_type=F32
            )
            inner = jnp.sum(probabilities * grad_probs, 0, keepdims=True)
            grad_scores = (probabilities * (grad_probs - inner)).astype(BF16)
            queries_t[columns, rows] = jnp.dot(
                keys_t[columns, :seen], grad_scores, preferred_element_type=F32
            )
            keys_sum[:seen, columns] += jnp.dot(grad_scores, query, preferred_element_type=F32)
            values_sum[:seen, columns] += jnp.dot(weights, grad, preferred_element_type=F32)
    out_ref[0] = outputs_t[...].T.astype(BF16)
    grad_query_ref[0] = (rot_back(queries_t[...].T) * scale).astype(BF16)
    grad_key_ref[0] = rot_back(keys_sum[...]).astype(BF16)
    grad_value_ref[0] = values_sum[...].astype(BF16)


def attention(projected, grad_attended, cosine, sine, starts):
    count, length, width = grad_attended.shape
    pairs = width // PAIR
    work = count * length * length * width
    return pl.pallas_call(
        attention_kernel,
        grid=(count, pairs),
        out_shape=(jax.ShapeDtypeStruct((count, length, width), BF16),) * 4,
        in_specs=[
            pl.BlockSpec((1, length, PAIR), lambda s, h: (s, 0, h)),
            pl.BlockSpec((1, length, PAIR), lambda s, h: (s, 0, h + pairs)),
            pl.BlockSpec((1, length, PAIR), lambda s, h: (s, 0, h + 2 * pairs)),
            pl.BlockSpec((1, length, PAIR), lambda s, h: (s, 0, h)),
            pl.BlockSpec((1, length, PAIR), lambda s, h: (s, 0, 0)),
            pl.BlockSpec((1, length, PAIR), lambda s, h: (s, 0, 0)),
            pl.BlockSpec((1, 1, length), lambda s, h: (s, 0, 0)),
        ],
        out_specs=(pl.BlockSpec((1, length, PAIR), lambda s, h: (s, 0, h)),) * 4,
        scratch_shapes=[
            pltpu.VMEM((PAIR, length), F32),
            pltpu.VMEM((PAIR, length), F32),
            pltpu.VMEM((length, PAIR), F32),
            pltpu.VMEM((length, PAIR), F32),
        ],
        compiler_params=pltpu.CompilerParams(vmem_limit_bytes=48 * 1024 * 1024),
        cost_estimate=pl.CostEstimate(
            flops=30 * work, bytes_accessed=24 * count * length * width,
            transcendentals=work // (2 * HEAD_DIM),
        ),
        name="attention",
    )(projected, projected, projected, grad_attended, cosine, sine, starts)


def make_shards(dp_size, tensor_size):
    def shards(
        hidden_in, segments, ln1_gain, ln1_bias, ln2_gain, ln2_bias, w_qkv, b_qkv,
        w_out, b_out, w_up, b_up, w_down, b_down, cotangent,
    ):
        count, own_length, width = hidden_in.shape
        length = segments.shape[1]
        rows = count * length
        dp_index, tensor_index = lax.axis_index("dp"), lax.axis_index("tensor")
        local = w_qkv.shape[2]
        local_units = w_up.shape[1]
        bits = bits_of(dp_size)
        order_a = bits[1:] + bits[:1]
        order_b = bits[:0:-1] + bits[:1]

        def gather(block):
            return gather_tokens(block, "tensor", tensor_size, tensor_index).reshape(rows, width)

        def scatter(parts, between=None):
            parts = parts.reshape(count, tensor_size, own_length, width)
            return scatter_tokens(parts, "tensor", tensor_size, tensor_index, between)

        hidden_rows = gather(hidden_in)
        attn_w = jnp.concatenate([w_qkv[0], w_qkv[1], w_qkv[2], w_out], 1)
        attn_full = gather_rows(attn_w, "dp", dp_size, dp_index, order_a).reshape(width, 4 * local)
        full_qkv, full_out = attn_full[:, : 3 * local], attn_full[:, 3 * local :]
        full_up = gather_rows(w_up, "dp", dp_size, dp_index, order_b).reshape(width, local_units)
        hidden_rows, later_cot = lax.optimization_barrier((hidden_rows, cotangent))
        cot_rows = gather(later_cot)
        full_down = gather_rows(w_down, "dp", dp_size, dp_index, order_a).reshape(width, local_units)

        zeros = jnp.sum((segments == 0).astype(jnp.int32), -1, keepdims=True)
        ones = jnp.sum((segments == 1).astype(jnp.int32), -1, keepdims=True)
        starts = jnp.where(segments >= 1, zeros, 0) + jnp.where(segments >= 2, ones, 0)
        positions = jnp.arange(length, dtype=jnp.int32)[None] - starts
        place = jnp.arange(PAIR, dtype=jnp.int32) % HEAD_DIM
        frequency = 10000.0 ** (-(place % (ROT // 2)).astype(F32) * (2.0 / ROT))
        angles = positions.astype(F32)[..., None] * frequency
        cosine = jnp.where(place < ROT, jnp.cos(angles), 1.0)
        sines = jnp.sin(angles)
        sine = jnp.where(place < ROT // 2, -sines, jnp.where(place < ROT, sines, 0.0))

        def layer_normed(hidden):
            centred = hidden - jnp.mean(hidden, -1, keepdims=True)
            scaling = lax.rsqrt(jnp.mean(centred * centred, -1, keepdims=True) + EPSILON)
            return centred * scaling, scaling

        normed, _ = layer_normed(hidden_rows.astype(F32))
        first = (normed * ln1_gain + ln1_bias).astype(BF16)
        second = (normed * ln2_gain + ln2_bias).astype(BF16)
        bias_qkv = lax.dynamic_slice_in_dim(b_qkv, tensor_index * local, local, 1)
        bias_up = lax.dynamic_slice_in_dim(b_up, tensor_index * local_units, local_units, 0)

        projected = jnp.dot(first, full_qkv, preferred_element_type=F32) + bias_qkv.reshape(-1)
        grad_attended = jnp.dot(cot_rows, full_out, preferred_element_type=F32).astype(BF16)
        attended, *grad_parts = attention(
            projected.reshape(count, length, 3 * local),
            grad_attended.reshape(count, length, local),
            cosine, sine, starts[:, None, :],
        )
        attended = attended.reshape(rows, local)
        grad_projected = jnp.concatenate(grad_parts, -1).reshape(rows, 3 * local)

        units = jnp.dot(second, full_up, preferred_element_type=F32) + bias_up
        cumulative = 0.5 * (1.0 + lax.erf(units * (1.0 / math.sqrt(2.0))))
        density = jnp.exp(-0.5 * units * units) * (1.0 / math.sqrt(2.0 * math.pi))
        activated = (units * cumulative).astype(BF16)
        slope = cumulative + units * density
        grad_units = (jnp.dot(cot_rows, full_down, preferred_element_type=F32) * slope).astype(BF16)

        branch = lax.dot_general(attended, full_out, BY_COLUMNS, preferred_element_type=F32)
        branch = branch + lax.dot_general(activated, full_down, BY_COLUMNS, preferred_element_type=F32)
        hidden = hidden_in.astype(F32)
        block_out = (hidden + scatter(branch) + b_out + b_down).astype(BF16)

        grad_first = lax.dot_general(grad_projected, full_qkv, BY_COLUMNS, preferred_element_type=F32)
        grad_second = lax.dot_general(grad_units, full_up, BY_COLUMNS, preferred_element_type=F32)
        norm_terms = [
            jnp.sum(grad_first * normed, 0), jnp.sum(grad_first, 0),
            jnp.sum(grad_second * normed, 0), jnp.sum(grad_second, 0),
        ]
        def to_owners(part, order):
            split = part.reshape((dp_size, part.shape[0] // dp_size) + part.shape[1:])
            return scatter_rows(split, "dp", dp_size, dp_index, bits[:1] + order)

        xy, yx = bits[1:], bits[:0:-1]
        grad_w_down = to_owners(lax.dot_general(cot_rows, activated, BY_ROWS, preferred_element_type=F32), xy)
        grad_w_up = to_owners(lax.dot_general(second, grad_units, BY_ROWS, preferred_element_type=F32), yx)
        attn_parts = jnp.concatenate([
            lax.dot_general(first, grad_projected, BY_ROWS, preferred_element_type=F32),
            lax.dot_general(cot_rows, attended, BY_ROWS, preferred_element_type=F32),
        ], 1)
        grad_attn = to_owners(attn_parts, yx)
        grad_w_out = grad_attn[:, 3 * local :]
        grad_w_qkv = jnp.stack([grad_attn[:, c * local : (c + 1) * local] for c in range(3)])

        padded_qkv = lax.dynamic_update_slice_in_dim(
            jnp.zeros((3, width), F32),
            jnp.sum(grad_projected, 0, dtype=F32).reshape(3, local), tensor_index * local, 1,
        )
        padded_up = lax.dynamic_update_slice_in_dim(
            jnp.zeros(b_up.shape, F32), jnp.sum(grad_units, 0, dtype=F32), tensor_index * local_units, 0
        )
        cot_sums = jnp.sum(cotangent, (0, 1), dtype=F32)
        vector = jnp.concatenate(norm_terms + [padded_qkv.reshape(-1), cot_sums, padded_up])
        vector = [vector.reshape(-1, 128)]
        stages = sum_stages((("tensor", tensor_size), ("dp", dp_size)))
        share = -(-len(stages) // (tensor_size - 1))

        def sum_some(step, left, right):
            for stage in stages[(step - 1) * share : step * share]:
                vector[0] = vector[0] + swapped(vector[0], *stage)
            left, right, vector[0] = lax.optimization_barrier((left, right, vector[0]))
            return left, right

        e = scatter(grad_first * ln1_gain + grad_second * ln2_gain, sum_some)
        own_normed, own_scaling = layer_normed(hidden)
        grad_in = cotangent.astype(F32) + own_scaling * (
            e
            - jnp.mean(e, -1, keepdims=True)
            - own_normed * jnp.mean(e * own_normed, -1, keepdims=True)
        )

        vector = vector[0].reshape(-1)
        g1, b1, g2, b2, qkv, cot_sum, up = jnp.split(
            vector, [width, 2 * width, 3 * width, 4 * width, 7 * width, 8 * width]
        )
        return (
            block_out, grad_in.astype(BF16), g1, b1, g2, b2, grad_w_qkv, qkv.reshape(3, width),
            grad_w_out, cot_sum, grad_w_up, up, grad_w_down, cot_sum,
        )

    return shards


def solution(mesh):
    tokens = P("dp", "tensor", None)
    weight = P("dp", "tensor")
    stacked = P(None, "dp", "tensor")
    in_specs = (
        tokens, P("dp", None), P(), P(), P(), P(), stacked, P(),
        weight, P(), weight, P(), weight, P(), tokens,
    )
    out_specs = (
        tokens, tokens, P(), P(), P(), P(), stacked, P(),
        weight, P(), weight, P(), weight, P(),
    )
    shards = make_shards(mesh.shape["dp"], mesh.shape["tensor"])
    return jax.shard_map(shards, mesh=mesh, in_specs=in_specs, out_specs=out_specs, check_vma=False)
```
